128 devices in a mesh: seq: 16 (over x, z_hi, core), tp: 8 (over z_lo, y).
Axes of the slice: x: 4, y: 4, z: 4 (z_hi: 2, z_lo: 2; z = z_hi * 2 + z_lo), core: 2. Of those that a mesh axis runs over, the one named last changes fastest.
Arguments:
- query_stream: bfloat16 [4096, 8192], P('seq', 'tp'), may hold values from -6 to 6
- key_stream: bfloat16 [4096, 8192], P('seq', 'tp'), may hold values from -6 to 6
- value_stream: bfloat16 [4096, 8192], P('seq', 'tp'), may hold values from -6 to 6
- decay_rate: float32 [8192, 16], P('tp'), may hold values from 0.00012207031 to 0.08
- residue: float32 [8192, 16], P('tp'), may hold values from -2 to 2
- skip_gain: float32 [8192], P('tp'), may hold values from -3 to 3
- out_weight: bfloat16 [8192, 8192], P('seq', 'tp'), may hold values from -0.0625 to 0.0625
Outputs:
- mixed: bfloat16 [4096, 8192], P('seq', 'tp')
The draws below stay inside these ranges and needn't reach their ends.
All inputs are finite; a program needn't handle non-finite values.
Results may differ from the reference program's by a relative error of at most 0.015.
Values may be sent and summed in bfloat16 or wider, within the bound.
A program may use at most 64 MiB of HBM per device.

```python
import math
import jax
import jax.numpy as jnp
from jax import lax

D = 8192
MODES = 16
SEQ_LEN = 4096


def steps_of(own_key, extent, pieces, low, largest):
    factor_of, own = 1.0, jax.random.fold_in(own_key, 6)
    for position, shards_of in pieces:
        heights = jnp.exp(jax.random.uniform(jax.random.fold_in(own, position), (shards_of,), jnp.float32, low / len(pieces), largest / len(pieces)))
        factor_of = factor_of * jnp.repeat(heights, extent[position] // shards_of).reshape([-1 if axis == position else 1 for axis in range(len(extent))])
    return factor_of


def normal_values(rng, extent, deviation, most, split=(), kind=jnp.bfloat16):
    entries = jax.random.normal(rng, extent, jnp.float32) * deviation
    if len(split) > 0:
        entries = steps_of(rng, extent, split, -0.22, 0.18) * entries
    return jnp.clip(entries, min=-most, max=most).astype(kind)


def setup_inputs(seed: int = 0) -> dict:
    splits = jax.random.split(jax.random.key(seed), 8)
    return {
        "query_stream": normal_values(splits[0], (SEQ_LEN, D), 1.0, 6.0, ((0, 16), (1, 8))),
        "key_stream": normal_values(splits[1], (SEQ_LEN, D), 1.0, 6.0, ((0, 16), (1, 8))),
        "value_stream": normal_values(splits[2], (SEQ_LEN, D), 1.0, 6.0, ((0, 16), (1, 8))),
        "decay_rate": jnp.clip(jnp.exp(math.log(0.08) - 6.4851847 * jax.random.uniform(splits[3], (D, MODES), jnp.float32) ** steps_of(splits[3], (D, MODES), ((0, 8),), -0.2, 0.2)), 0.00012207031, 0.08),
        "residue": normal_values(splits[4], (D, MODES), 0.35, 2.0, ((0, 8),), jnp.float32),
        "skip_gain": normal_values(splits[5], (D,), 0.6, 3.0, ((0, 8),), jnp.float32),
        "out_weight": normal_values(splits[6], (D, D), D ** -0.5, 0.0625, ((0, 16), (1, 8))),
    }


def reference(query_stream, key_stream, value_stream, decay_rate, residue, skip_gain, out_weight):
    product = (key_stream.astype(jnp.float32) * value_stream.astype(jnp.float32)).astype(jnp.bfloat16)
    steps = jnp.arange(SEQ_LEN).astype(jnp.float32)
    coef = residue * jnp.sqrt(-jnp.expm1(-2.0 * decay_rate))
    group = min(D, 256)
    source = product.astype(jnp.float32).T.reshape(D // group, group, SEQ_LEN)
    rates = decay_rate.reshape(D // group, group, MODES)
    coefs = coef.reshape(D // group, group, MODES)

    def convolve(items):
        signal, rate, weight = items
        taps = jnp.einsum('gm,gmt->gt', weight, jnp.exp(-rate[:, :, None] * steps[None, None, :]))
        length = 2 * SEQ_LEN
        spectrum = jnp.fft.rfft(signal, length, axis=1) * jnp.fft.rfft(taps, length, axis=1)
        return jnp.fft.irfft(spectrum, length, axis=1)[:, :SEQ_LEN]
    along = lax.map(convolve, (source, rates, coefs)).reshape(D, SEQ_LEN).T
    convolved = (along + skip_gain[None, :] * product.astype(jnp.float32)).astype(jnp.bfloat16)
    gated = (query_stream.astype(jnp.float32) * convolved.astype(jnp.float32)).astype(jnp.bfloat16)
    return jnp.dot(gated, out_weight, preferred_element_type=jnp.float32).astype(jnp.bfloat16)
```

```python
import functools

import jax
import jax.numpy as jnp
from jax import lax
from jax.experimental import pallas as pl
from jax.experimental.pallas import tpu as pltpu
from jax.sharding import PartitionSpec as P

MESH = pl.DeviceIdType.MESH
F32, BF16 = jnp.float32, jnp.bfloat16

ROWS, CHAN, KROWS, MODES = 256, 1024, 512, 16
SEG = ROWS // 8
LANES = 128
GROUPS = CHAN // LANES

PIECE = 64
NP = KROWS // PIECE
ZFIRST = 6
AHEAD = 2

X_RIGHT = (
    [(0, 0, p) for p in range(8)]
    + [(0, 1, 0), (-1, 0, 6)]
    + [(0, 1, p) for p in range(1, ZFIRST)]
    + [(-1, 0, p) for p in (0, 2, 4)]
    + [(-1, 1, p) for p in (0, 2, 4)]
)
X_LEFT = (
    [(0, 0, p) for p in range(8)]
    + [(0, 1, 0), (1, 0, 7)]
    + [(0, 1, p) for p in range(1, ZFIRST)]
    + [(1, 0, p) for p in (1, 3, 5)]
    + [(1, 1, p) for p in (1, 3, 5)]
)
Z_SEND = [(0, 0, p) for p in range(8)] + [None, None] + [(-1, 0, 6), (-1, 0, 7), (1, 0, 6), (1, 0, 7), (2, 0, 6), (2, 0, 7)]
NX, NZ = len(X_RIGHT), len(Z_SEND)

GP = 256
Y_RIGHT = [(0, 0, p) for p in range(4)] + [(0, 1, p) for p in range(4)] + [(-1, 0, 0), (-1, 0, 2), (-1, 1, 0), (-1, 1, 2)]
Y_LEFT = [(0, 0, p) for p in range(4)] + [(0, 1, p) for p in range(4)] + [(1, 0, 1), (1, 0, 3), (1, 1, 1), (1, 1, 3)]
NY = len(Y_RIGHT)


def expm1(u):
    series = jnp.ones_like(u)
    for n in range(8, 1, -1):
        series = 1.0 + series * u * (1.0 / n)
    return jnp.where(u > -0.3, u * series, jnp.exp(u) - 1.0)


def kernel(q_hbm, k_hbm, v_hbm, rate_hbm, res_hbm, skip_hbm, w_hbm, out_ref,
           q, k, v, rate, res, skip, wbuf, gbuf, acc, prod, conv, lam_b, coef_b, starts,
           e_own, e_sib, e_chip, e_in, s_in, lam_block,
           in_sem, own_sem, s_xr, r_xr, s_xl, r_xl, s_z, r_z, s_w, r_w, s_yr, r_yr, s_yl, r_yl, s_g, r_g,
           s_e, r_e, s_st, r_st):
    s, t = lax.axis_index("seq"), lax.axis_index("tp")
    x, zh, c = s // 4, (s // 2) % 2, s % 2
    zl, y = t // 4, t % 4
    j = s // 2

    def at(dx=0, dzh=0, dc=0, dy=0, dzl=0):
        x2, zh2, c2 = (x + dx + 4) % 4, (zh + dzh) % 2, (c + dc) % 2
        return ((x2 * 2 + zh2) * 2 + c2, ((zl + dzl) % 2) * 4 + (y + dy + 4) % 4)

    def chip_block(dx, dz):
        return ((x + dx + 4) % 4) * 2 + (zh + dz) % 2

    def remote(src, dst, ssem, rsem, device):
        return pltpu.make_async_remote_copy(
            src_ref=src, dst_ref=dst, send_sem=ssem, recv_sem=rsem, device_id=device, device_id_type=MESH
        )

    ins = [
        pltpu.make_async_copy(a, b, in_sem.at[i])
        for i, (a, b) in enumerate(
            ((k_hbm, k), (v_hbm, v), (rate_hbm, rate), (res_hbm, res), (skip_hbm, skip), (q_hbm, q))
        )
    ]
    for cp in ins:
        cp.start()
    partners = [at(dc=1), at(dy=1), at(dy=3), at(dzl=1)] + [
        at(dx=a, dzh=b) for a in range(4) for b in range(2) if (a, b) != (0, 0)
    ]
    barrier = pltpu.get_barrier_semaphore()
    for device in partners:
        pl.semaphore_signal(barrier, inc=1, device_id=device, device_id_type=MESH)

    for cp in ins:
        cp.wait()
    rate_t, res_t = rate[...].T, res[...].T
    lam_t = jnp.exp(-rate_t)
    coef_t = res_t * jnp.sqrt(-expm1(-2.0 * rate_t))
    for m in range(MODES):
        lam_b[m] = jnp.broadcast_to(lam_t[m : m + 1, :], (8, CHAN))
        coef_b[m] = jnp.broadcast_to(coef_t[m : m + 1, :], (8, CHAN))
    lam_block[...] = jnp.exp(-float(ROWS) * rate_t)
    pl.semaphore_wait(barrier, len(partners))

    sent = []

    def start(copy):
        copy.start()
        sent.append(copy)

    have = {(0, 0, p) for p in range(NP)}

    def piece(item):
        dx, dz, p = item
        return wbuf.at[chip_block(dx, dz) * 2 + c, pl.ds(p * PIECE, PIECE)]

    def source(item):
        dx, dz, p = item
        if (dx % 4, dz) == (0, 0):
            return w_hbm.at[pl.ds(p * PIECE, PIECE)]
        assert (dx % 4, dz, p) in have
        return piece(item)

    links = (
        (X_RIGHT, s_xr, r_xr, dict(dx=1), -1, 0),
        (X_LEFT, s_xl, r_xl, dict(dx=3), 1, 0),
        (Z_SEND, s_z, r_z, dict(dzh=1), 0, 1),
    )

    def issue(r):
        for items, ssem, rsem, where, _, _ in links:
            if r < len(items) and items[r] is not None:
                start(remote(source(items[r]), piece(items[r]), ssem.at[r], rsem.at[r], at(**where)))

    order = []

    def absorb(r):
        for items, ssem, rsem, where, ox, oz in links:
            if r < len(items) and items[r] is not None:
                dx, dz, p = items[r]
                item = ((dx + ox) % 4, (dz + oz) % 2, p)
                assert item not in have
                have.add(item)
                remote(piece(item), piece(item), ssem.at[r], rsem.at[r], at(**where)).wait_recv()
                n = len(order)
                order.append(item)
                start(remote(piece(item), piece(item), s_w.at[n], r_w.at[n], at(dc=1)))
        issue(r + AHEAD)

    def sibling_piece(item):
        dx, dz, p = item
        return wbuf.at[chip_block(dx, dz) * 2 + 1 - c, pl.ds(p * PIECE, PIECE)]

    taken = [0]

    def from_sibling(count):
        while taken[0] < count:
            n = taken[0]
            ref = sibling_piece(order[n])
            remote(ref, ref, s_w.at[n], r_w.at[n], at(dc=1)).wait_recv()
            taken[0] += 1

    for r in range(AHEAD):
        issue(r)
    own = wbuf.at[s]
    own_in = pltpu.make_async_copy(w_hbm, own, own_sem)
    own_in.start()
    start(remote(w_hbm, own, s_e.at[1], r_e.at[1], at(dc=1)))

    for g in range(GROUPS):
        lanes = pl.ds(g * LANES, LANES)
        prod[g] = (k[:, lanes].astype(F32) * v[:, lanes].astype(F32)).astype(BF16).astype(F32)
    seg_at = lax.broadcasted_iota(jnp.int32, (MODES, 8, LANES), 1)
    for g in range(GROUPS):
        lanes = pl.ds(g * LANES, LANES)
        lam = lam_b[:, :, lanes]

        def ends(i, state):
            return lam * state + prod[g, pl.ds(i, 8, stride=SEG), :][None]

        state = lax.fori_loop(0, SEG, ends, jnp.zeros((MODES, 8, LANES), F32), unroll=4)
        power = lam
        for _ in range(5):
            power = power * power
        scan = state
        for step in (1, 2, 4):
            moved = jnp.where(seg_at >= step, pltpu.roll(scan, step, 1), 0.0)
            scan = scan + power * moved
            power = power * power
        starts[:, :, lanes] = jnp.where(seg_at >= 1, pltpu.roll(scan, 1, 1), 0.0)
        for m in range(MODES):
            e_own[pl.ds(m, 1), lanes] = scan[m, 7:8, :]

    pass_e = remote(e_own, e_sib, s_e.at[0], r_e.at[0], at(dc=1))
    start(pass_e)
    pass_e.wait_recv()
    half = pl.ds(pl.multiple_of(8 * c, 8), 8)
    lam_h = lam_block[half, :]
    mine, other = e_own[half, :], e_sib[half, :]
    e_chip[...] = jnp.where(c == 0, lam_h * mine + other, lam_h * other + mine)
    later = []
    for d in range(1, 8):
        j2 = j + d
        device = ((j2 % 8) * 2 + c, t)
        later.append((j2 < 8, remote(e_chip, e_in.at[j], s_st.at[d], r_st.at[j], device)))
    for ok, copy in later:
        pl.when(ok)(copy.start)
    absorb(0)
    s_half = s_in.at[half, :]
    s_half[...] = jnp.zeros((8, CHAN), F32)
    lam2 = lam_h * lam_h
    for j1 in range(7):

        @pl.when(j1 < j)
        def _(j1=j1):
            remote(e_chip, e_in.at[j1], s_st.at[0], r_st.at[j1], at(dc=1)).wait_recv()
            s_half[...] = lam2 * s_half[...] + e_in[j1]

    pass_s = remote(s_half, s_half, s_e.at[2], r_e.at[2], at(dc=1))
    start(pass_s)
    pass_s_in = s_in.at[pl.ds(pl.multiple_of(8 - 8 * c, 8), 8), :]
    remote(pass_s_in, pass_s_in, s_e.at[2], r_e.at[2], at(dc=1)).wait_recv()
    absorb(1)

    have_g = set()

    def g_piece(item):
        dy, dz, p = item
        return gbuf.at[((zl + dz) % 2) * 4 + (y + dy + 4) % 4, :, pl.ds(p * GP, GP)]

    g_links = ((Y_RIGHT, s_yr, r_yr, dict(dy=1), -1), (Y_LEFT, s_yl, r_yl, dict(dy=3), 1))

    def issue_g(r):
        for items, ssem, rsem, where, _ in g_links:
            if r < NY:
                dy, dz, p = items[r]
                assert (dy % 4, dz, p) in have_g
                start(remote(g_piece(items[r]), g_piece(items[r]), ssem.at[r], rsem.at[r], at(**where)))

    def absorb_zl(p):
        ref = g_piece((0, 1, p))
        remote(ref, ref, s_g.at[p], r_g.at[p], at(dzl=1)).wait_recv()
        have_g.add((0, 1, p))

    def absorb_g(r):
        if r >= NY:
            return
        for items, ssem, rsem, where, oy in g_links:
            dy, dz, p = items[r]
            item = ((dy + oy) % 4, dz, p)
            ref = g_piece(item)
            remote(ref, ref, ssem.at[r], rsem.at[r], at(**where)).wait_recv()
            assert item not in have_g
            have_g.add(item)
        issue_g(r + AHEAD)

    before = jnp.where(c == 0, s_in[...], lam_block[...] * s_in[...] + e_sib[...])
    e_own_state = before
    row_seg = lax.broadcasted_iota(jnp.int32, (8, LANES), 0).astype(F32)
    for g in range(GROUPS):
        lanes = pl.ds(g * LANES, LANES)
        lam, coef = lam_b[:, :, lanes], coef_b[:, :, lanes]
        power = lam
        for _ in range(5):
            power = power * power
        lift = jnp.where(seg_at % 2 == 1, power, 1.0)
        power = power * power
        lift = lift * jnp.where((seg_at // 2) % 2 == 1, power, 1.0)
        power = power * power
        lift = lift * jnp.where(seg_at // 4 == 1, power, 1.0)
        first = jnp.stack([jnp.broadcast_to(e_own_state[m : m + 1, g * LANES : (g + 1) * LANES], (8, LANES)) for m in range(MODES)])
        gain = skip[:, lanes]

        def step(i, state):
            p = prod[g, pl.ds(i, 8, stride=SEG), :]
            state = lam * state + p[None]
            conv[g, pl.ds(i, 8, stride=SEG), :] = jnp.sum(coef * state, axis=0) + gain * p
            return state

        lax.fori_loop(0, SEG, step, starts[:, :, lanes] + lift * first, unroll=4)
        rounded = conv[g].astype(BF16).astype(F32)
        gbuf[t, :, lanes] = (q[:, lanes].astype(F32) * rounded).astype(BF16)
        if g % 2 == 1:
            p = g // 2
            have_g.add((0, 0, p))
            ref = g_piece((0, 0, p))
            start(remote(ref, ref, s_g.at[p], r_g.at[p], at(dzl=1)))
            if p < AHEAD:
                issue_g(p)
            if p == 1:
                absorb(2)

    g_base = 3
    for r in range(g_base, g_base + NY):
        rg = r - g_base
        absorb(r)
        if rg < 4:
            absorb_zl(rg)
        absorb_g(rg)
    at_round = g_base + NY

    own_in.wait()
    remote(w_hbm, wbuf.at[s + 1 - 2 * c], s_e.at[1], r_e.at[1], at(dc=1)).wait_recv()

    def multiply(dx, dz, first=False):
        b = chip_block(dx, dz)

        @pl.loop(0, CHAN, step=256)
        def _(n):
            cols = pl.ds(pl.multiple_of(n, 256), 256)
            w = wbuf[pl.ds(2 * b, 2), :, cols].reshape(2 * KROWS, 256)
            part = jnp.dot(gbuf[b], w, preferred_element_type=F32)
            acc[:, cols] = part if first else acc[:, cols] + part

    def complete(n):
        return sum(1 for item in order[:n])

    done = set()

    def ready():
        names = [(0, 0), (1, 0), (3, 0), (0, 1), (1, 1), (3, 1), (2, 0), (2, 1)]
        return [b for b in names if b not in done and all((*b, p) in have for p in range(NP))]

    def last_of(b):
        return max((i + 1 for i, item in enumerate(order) if item[:2] == b), default=0)

    for r in range(at_round, NX):
        todo = ready()[:2]
        for b in todo:
            from_sibling(last_of(b))
            multiply(*b, first=not done)
            done.add(b)
        absorb(r)
    for b in ready():
        from_sibling(last_of(b))
        multiply(*b, first=not done)
        done.add(b)
    from_sibling(len(order))
    assert len(done) == 8
    out_ref[...] = acc[...].astype(BF16)

    for copy in sent:
        copy.wait_send()
    for ok, copy in later:
        pl.when(ok)(copy.wait_send)


def body(query_stream, key_stream, value_stream, decay_rate, residue, skip_gain, out_weight):
    dma = pltpu.SemaphoreType.DMA
    n_w = 2 * NX + sum(i is not None for i in Z_SEND)
    vm = pltpu.VMEM
    return pl.pallas_call(
        kernel,
        out_shape=jax.ShapeDtypeStruct((ROWS, CHAN), BF16),
        in_specs=[pl.BlockSpec(memory_space=pl.ANY)] * 7,
        out_specs=pl.BlockSpec(memory_space=pltpu.VMEM),
        scratch_shapes=[
            vm((ROWS, CHAN), BF16), vm((ROWS, CHAN), BF16), vm((ROWS, CHAN), BF16),
            vm((CHAN, MODES), F32), vm((CHAN, MODES), F32), vm((1, CHAN), F32),
            vm((16, KROWS, CHAN), BF16), vm((8, ROWS, CHAN), BF16), vm((ROWS, CHAN), F32),
            vm((GROUPS, ROWS, LANES), F32), vm((GROUPS, ROWS, LANES), F32),
            vm((MODES, 8, CHAN), F32), vm((MODES, 8, CHAN), F32), vm((MODES, 8, CHAN), F32),
            vm((MODES, CHAN), F32), vm((MODES, CHAN), F32), vm((8, CHAN), F32), vm((7, 8, CHAN), F32),
            vm((MODES, CHAN), F32), vm((MODES, CHAN), F32),
            dma((6,)), dma, dma((NX,)), dma((NX,)), dma((NX,)), dma((NX,)), dma((NZ,)), dma((NZ,)),
            dma((n_w,)), dma((n_w,)), dma((NY,)), dma((NY,)), dma((NY,)), dma((NY,)), dma((4,)), dma((4,)),
            dma((3,)), dma((3,)), dma((8,)), dma((8,)),
        ],
        compiler_params=pltpu.CompilerParams(
            collective_id=0, has_side_effects=True, vmem_limit_bytes=56 << 20
        ),
        cost_estimate=pl.CostEstimate(flops=2 * ROWS * 8192 * CHAN, bytes_accessed=4 << 20, transcendentals=0),
        name="hyena",
    )(query_stream, key_stream, value_stream, decay_rate, residue, skip_gain[None], out_weight)


def solution(mesh):
    placed = (
        P("seq", "tp"),
        P("seq", "tp"),
        P("seq", "tp"),
        P("tp", None),
        P("tp", None),
        P("tp"),
        P("seq", "tp"),
    )
    return jax.shard_map(
        body, mesh=mesh, in_specs=placed, out_specs=P("seq", "tp"), check_vma=False
    )
```

```python
import functools

import jax
import jax.numpy as jnp
from jax import lax
from jax.experimental import pallas as pl
from jax.experimental.pallas import tpu as pltpu
from jax.sharding import PartitionSpec as P

MESH = pl.DeviceIdType.MESH
F32, BF16 = jnp.float32, jnp.bfloat16

ROWS, CHAN, KROWS, MODES = 256, 1024, 512, 16
SEG = ROWS // 8
LANES = 128
GROUPS = CHAN // LANES

PIECE = 64
NP = KROWS // PIECE
ZFIRST = 6
EARLY = 2
G_BASE = 5

X_RIGHT = (
    [(0, 0, p) for p in range(8)]
    + [(0, 1, 0), (0, 1, 1), (0, 1, 2), (-1, 0, 6)]
    + [(0, 1, p) for p in range(3, ZFIRST)]
    + [(-1, 0, p) for p in (0, 2, 4)]
    + [(-1, 1, p) for p in (0, 2, 4)]
)
X_LEFT = (
    [(0, 0, p) for p in range(8)]
    + [(0, 1, 0), (0, 1, 1), (0, 1, 2), (1, 0, 7)]
    + [(0, 1, p) for p in range(3, ZFIRST)]
    + [(1, 0, p) for p in (1, 3, 5)]
    + [(1, 1, p) for p in (1, 3, 5)]
)
Z_EARLY = 5
Z_SEND = (
    [(0, 0, p) for p in range(Z_EARLY)]
    + [None] * 4
    + [(0, 0, p) for p in range(Z_EARLY, 8)]
    + [(-1, 0, 6), (-1, 0, 7), (1, 0, 6), (1, 0, 7), (2, 0, 6), (2, 0, 7)]
)
NX, NZ = len(X_RIGHT), len(Z_SEND)

GP = 256
Y_RIGHT = [(0, 0, p) for p in range(4)] + [(0, 1, p) for p in range(4)] + [(-1, 0, 0), (-1, 0, 2), (-1, 1, 0), (-1, 1, 2)]
Y_LEFT = [(0, 0, p) for p in range(4)] + [(0, 1, p) for p in range(4)] + [(1, 0, 1), (1, 0, 3), (1, 1, 1), (1, 1, 3)]
NY = len(Y_RIGHT)


def expm1(u):
    series = jnp.ones_like(u)
    for n in range(8, 1, -1):
        series = 1.0 + series * u * (1.0 / n)
    return jnp.where(u > -0.3, u * series, jnp.exp(u) - 1.0)


def kernel(q_hbm, k_hbm, v_hbm, rate_hbm, res_hbm, skip_hbm, w_hbm, out_ref,
           q, k, v, rate, res, skip, wbuf, gbuf, acc, prod, conv, lam_b, coef_b, starts,
           e_own, e_sib, e_chip, e_in, s_in, lam_block,
           in_sem, own_sem, r_xr, r_xl, r_z, s_w, r_w, r_yr, r_yl, s_g, r_g,
           s_e, r_e, s_st, r_st):
    s, t = lax.axis_index("seq"), lax.axis_index("tp")
    x, zh, c = s // 4, (s // 2) % 2, s % 2
    zl, y = t // 4, t % 4
    j = s // 2

    def at(dx=0, dzh=0, dc=0, dy=0, dzl=0):
        x2, zh2, c2 = (x + dx + 4) % 4, (zh + dzh) % 2, (c + dc) % 2
        return ((x2 * 2 + zh2) * 2 + c2, ((zl + dzl) % 2) * 4 + (y + dy + 4) % 4)

    def chip_block(dx, dz):
        return ((x + dx + 4) % 4) * 2 + (zh + dz) % 2

    def remote(src, dst, ssem, rsem, device):
        return pltpu.make_async_remote_copy(
            src_ref=src, dst_ref=dst, send_sem=ssem, recv_sem=rsem, device_id=device, device_id_type=MESH
        )

    ins = [
        pltpu.make_async_copy(a, b, in_sem.at[i])
        for i, (a, b) in enumerate(
            ((k_hbm, k), (v_hbm, v), (rate_hbm, rate), (res_hbm, res), (skip_hbm, skip), (q_hbm, q))
        )
    ]
    for cp in ins:
        cp.start()
    partners = [at(dc=1), at(dy=1), at(dy=3), at(dzl=1)] + [
        at(dx=a, dzh=b) for a in range(4) for b in range(2) if (a, b) != (0, 0)
    ]
    barrier = pltpu.get_barrier_semaphore()
    for device in partners:
        pl.semaphore_signal(barrier, inc=1, device_id=device, device_id_type=MESH)

    pl.semaphore_wait(barrier, len(partners))

    pieces_out = [0]
    gated_out = [0]
    sent = []

    def start(copy):
        copy.start()
        sent.append(copy)

    have = {(0, 0, p) for p in range(NP)}

    def piece(item):
        dx, dz, p = item
        return wbuf.at[chip_block(dx, dz) * 2 + c, pl.ds(p * PIECE, PIECE)]

    def source(item):
        dx, dz, p = item
        if (dx % 4, dz) == (0, 0):
            return w_hbm.at[pl.ds(p * PIECE, PIECE)]
        assert (dx % 4, dz, p) in have
        return piece(item)

    links = (
        (X_RIGHT, r_xr, dict(dx=1), -1, 0),
        (X_LEFT, r_xl, dict(dx=3), 1, 0),
        (Z_SEND, r_z, dict(dzh=1), 0, 1),
    )

    issued = [0] * len(links)

    limits = [EARLY, EARLY, EARLY]

    def issue():
        for i, (items, rsem, where, _, _) in enumerate(links):
            while issued[i] < min(limits[i], len(items)):
                r = issued[i]
                if items[r] is not None:
                    dx, dz, p = items[r]
                    if (dx % 4, dz, p) not in have:
                        break
                    remote(source(items[r]), piece(items[r]), s_w, rsem.at[r], at(**where)).start()
                    pieces_out[0] += 1
                issued[i] += 1

    def absorb(r):
        for items, rsem, where, ox, oz in links:
            if r < len(items) and items[r] is not None:
                dx, dz, p = items[r]
                item = ((dx + ox) % 4, (dz + oz) % 2, p)
                assert item not in have
                have.add(item)
                ref = piece(item)
                remote(ref, ref, s_w, rsem.at[r], at(**where)).wait_recv()
                remote(ref, ref, s_w, r_w.at[group(item)], at(dc=1)).start()
                pieces_out[0] += 1
        issue()

    def group(item):
        dx, dz, p = item
        return dx * 2 + dz + (4 if (dx, dz) == (2, 1) and p >= NP // 2 else 0)

    def from_sibling(dx, dz, part=None):
        rows = KROWS if part is None else KROWS // 2
        first = (part or 0) * rows
        ref = wbuf.at[chip_block(dx, dz) * 2 + 1 - c, pl.ds(first, rows)]
        remote(ref, ref, s_w, r_w.at[group((dx, dz, first // PIECE))], at(dc=1)).wait_recv()

    issue()
    own = wbuf.at[s]
    own_in = pltpu.make_async_copy(w_hbm, own, own_sem)
    own_in.start()
    start(remote(w_hbm, own, s_e.at[1], r_e.at[1], at(dc=1)))

    for cp in ins:
        cp.wait()
    rate_t, res_t = rate[...], res[...]
    lam_t = jnp.exp(-rate_t)
    coef_t = res_t * jnp.sqrt(-expm1(-2.0 * rate_t))
    for m in range(MODES):
        lam_b[m] = jnp.broadcast_to(lam_t[m : m + 1, :], (8, CHAN))
        coef_b[m] = jnp.broadcast_to(coef_t[m : m + 1, :], (8, CHAN))
    lam_block[...] = jnp.exp(-float(ROWS) * rate_t)

    for g in range(GROUPS):
        lanes = pl.ds(g * LANES, LANES)
        prod[g] = (k[:, lanes].astype(F32) * v[:, lanes].astype(F32)).astype(BF16).astype(F32)
    seg_at = lax.broadcasted_iota(jnp.int32, (MODES, 8, LANES), 1)
    for g in range(GROUPS):
        lanes = pl.ds(g * LANES, LANES)
        lam = lam_b[:, :, lanes]

        def ends(i, state):
            return lam * state + prod[g, pl.ds(i, 8, stride=SEG), :][None]

        state = lax.fori_loop(0, SEG, ends, jnp.zeros((MODES, 8, LANES), F32), unroll=4)
        power = lam
        for _ in range(5):
            power = power * power
        scan = state
        for step in (1, 2, 4):
            moved = jnp.where(seg_at >= step, pltpu.roll(scan, step, 1), 0.0)
            scan = scan + power * moved
            power = power * power
        starts[:, :, lanes] = jnp.where(seg_at >= 1, pltpu.roll(scan, 1, 1), 0.0)
        for m in range(MODES):
            e_own[pl.ds(m, 1), lanes] = scan[m, 7:8, :]

    pass_e = remote(e_own, e_sib, s_e.at[0], r_e.at[0], at(dc=1))
    start(pass_e)
    pass_e.wait_recv()
    half = pl.ds(pl.multiple_of(8 * c, 8), 8)
    lam_h = lam_block[half, :]
    mine, other = e_own[half, :], e_sib[half, :]
    e_chip[...] = jnp.where(c == 0, lam_h * mine + other, lam_h * other + mine)
    later = []
    for d in range(1, 8):
        j2 = j + d
        device = ((j2 % 8) * 2 + c, t)
        later.append((j2 < 8, remote(e_chip, e_in.at[j], s_st.at[d], r_st.at[j], device)))
    for ok, copy in later:
        pl.when(ok)(copy.start)
    limits[:] = [NX, NX, Z_EARLY]
    absorb(0)
    s_half = s_in.at[half, :]
    s_half[...] = jnp.zeros((8, CHAN), F32)
    lam2 = lam_h * lam_h
    for j1 in range(7):

        @pl.when(j1 < j)
        def _(j1=j1):
            remote(e_chip, e_in.at[j1], s_st.at[0], r_st.at[j1], at(dc=1)).wait_recv()
            s_half[...] = lam2 * s_half[...] + e_in[j1]

    pass_s = remote(s_half, s_half, s_e.at[2], r_e.at[2], at(dc=1))
    start(pass_s)
    pass_s_in = s_in.at[pl.ds(pl.multiple_of(8 - 8 * c, 8), 8), :]
    remote(pass_s_in, pass_s_in, s_e.at[2], r_e.at[2], at(dc=1)).wait_recv()
    absorb(1)

    have_g = set()

    def g_piece(item):
        dy, dz, p = item
        return gbuf.at[((zl + dz) % 2) * 4 + (y + dy + 4) % 4, :, pl.ds(p * GP, GP)]

    g_links = ((Y_RIGHT, r_yr, dict(dy=1), -1), (Y_LEFT, r_yl, dict(dy=3), 1))

    issued_g = [0] * len(g_links)

    def issue_g():
        for i, (items, rsem, where, _) in enumerate(g_links):
            while issued_g[i] < NY:
                r = issued_g[i]
                dy, dz, p = items[r]
                if (dy % 4, dz, p) not in have_g:
                    break
                ref = g_piece(items[r])
                remote(ref, ref, s_g, rsem.at[r], at(**where)).start()
                gated_out[0] += 1
                issued_g[i] += 1

    def absorb_zl(p):
        ref = g_piece((0, 1, p))
        remote(ref, ref, s_g, r_g.at[p], at(dzl=1)).wait_recv()
        have_g.add((0, 1, p))
        issue_g()

    def absorb_g(r):
        if r >= NY:
            return
        for items, rsem, where, oy in g_links:
            dy, dz, p = items[r]
            item = ((dy + oy) % 4, dz, p)
            ref = g_piece(item)
            remote(ref, ref, s_g, rsem.at[r], at(**where)).wait_recv()
            assert item not in have_g
            have_g.add(item)
        issue_g()

    before = jnp.where(c == 0, s_in[...], lam_block[...] * s_in[...] + e_sib[...])
    e_own_state = before
    row_seg = lax.broadcasted_iota(jnp.int32, (8, LANES), 0).astype(F32)
    for g in range(GROUPS):
        lanes = pl.ds(g * LANES, LANES)
        lam, coef = lam_b[:, :, lanes], coef_b[:, :, lanes]
        power = lam
        for _ in range(5):
            power = power * power
        lift = jnp.where(seg_at % 2 == 1, power, 1.0)
        power = power * power
        lift = lift * jnp.where((seg_at // 2) % 2 == 1, power, 1.0)
        power = power * power
        lift = lift * jnp.where(seg_at // 4 == 1, power, 1.0)
        first = jnp.stack([jnp.broadcast_to(e_own_state[m : m + 1, g * LANES : (g + 1) * LANES], (8, LANES)) for m in range(MODES)])
        gain = skip[:, lanes]

        def step(i, state):
            p = prod[g, pl.ds(i, 8, stride=SEG), :]
            state = lam * state + p[None]
            conv[g, pl.ds(i, 8, stride=SEG), :] = jnp.sum(coef * state, axis=0) + gain * p
            return state

        lax.fori_loop(0, SEG, step, starts[:, :, lanes] + lift * first, unroll=4)
        rounded = conv[g].astype(BF16).astype(F32)
        gbuf[t, :, lanes] = (q[:, lanes].astype(F32) * rounded).astype(BF16)
        if g % 2 == 1:
            p = g // 2
            have_g.add((0, 0, p))
            ref = g_piece((0, 0, p))
            remote(ref, ref, s_g, r_g.at[p], at(dzl=1)).start()
            gated_out[0] += 1
            issue_g()
            if p == 1:
                absorb(2)

    limits[2] = NZ
    issue()
    for r in range(3, G_BASE + NY):
        absorb(r)
        rg = r - G_BASE
        if 0 <= rg < 4:
            absorb_zl(rg)
        if 0 <= rg:
            absorb_g(rg)

    own_in.wait()
    remote(w_hbm, wbuf.at[s + 1 - 2 * c], s_e.at[1], r_e.at[1], at(dc=1)).wait_recv()

    def multiply(dx, dz, part=None, first=False):
        b = chip_block(dx, dz)
        rows = KROWS if part is None else KROWS // 2
        at_row = (part or 0) * rows

        @pl.loop(0, CHAN, step=256)
        def _(n):
            cols = pl.ds(pl.multiple_of(n, 256), 256)
            if part is None:
                w = wbuf[pl.ds(2 * b, 2), :, cols].reshape(2 * KROWS, 256)
                total = jnp.dot(gbuf[b], w, preferred_element_type=F32)
            else:
                total = sum(
                    jnp.dot(
                        gbuf[b, :, pl.ds(h * KROWS + at_row, rows)],
                        wbuf[2 * b + h, pl.ds(at_row, rows), cols],
                        preferred_element_type=F32,
                    )
                    for h in range(2)
                )
            acc[:, cols] = total if first else acc[:, cols] + total

    done = set()
    blocks = [(0, 0), (1, 0), (3, 0), (0, 1), (1, 1), (3, 1), (2, 0)]

    def work(most):
        for b in [b for b in blocks if b not in done and all((*b, p) in have for p in range(NP))][:most]:
            if b != (0, 0):
                from_sibling(*b)
            multiply(*b, first=not done)
            done.add(b)

    for r in range(G_BASE + NY, NX):
        work(2)
        absorb(r)
    work(8)
    assert len(done) == 7
    for part in range(2):
        from_sibling(2, 1, part)
        multiply(2, 1, part)
    out_ref[...] = acc[...].astype(BF16)

    for copy in sent:
        copy.wait_send()
    assert pieces_out[0] * PIECE % KROWS == 0 and gated_out[0] % 4 == 0
    ref = wbuf.at[pl.ds(0, pieces_out[0] * PIECE // KROWS)]
    remote(ref, ref, s_w, r_w.at[0], at(dc=1)).wait_send()
    ref = gbuf.at[pl.ds(0, gated_out[0] // 4)]
    remote(ref, ref, s_g, r_g.at[0], at(dc=1)).wait_send()
    for ok, copy in later:
        pl.when(ok)(copy.wait_send)


def body(query_stream, key_stream, value_stream, decay_rate, residue, skip_gain, out_weight):
    dma = pltpu.SemaphoreType.DMA
    vm = pltpu.VMEM
    return pl.pallas_call(
        kernel,
        out_shape=jax.ShapeDtypeStruct((ROWS, CHAN), BF16),
        in_specs=[pl.BlockSpec(memory_space=pl.ANY)] * 7,
        out_specs=pl.BlockSpec(memory_space=pltpu.VMEM),
        scratch_shapes=[
            vm((ROWS, CHAN), BF16), vm((ROWS, CHAN), BF16), vm((ROWS, CHAN), BF16),
            vm((MODES, CHAN), F32), vm((MODES, CHAN), F32), vm((1, CHAN), F32),
            vm((16, KROWS, CHAN), BF16), vm((8, ROWS, CHAN), BF16), vm((ROWS, CHAN), F32),
            vm((GROUPS, ROWS, LANES), F32), vm((GROUPS, ROWS, LANES), F32),
            vm((MODES, 8, CHAN), F32), vm((MODES, 8, CHAN), F32), vm((MODES, 8, CHAN), F32),
            vm((MODES, CHAN), F32), vm((MODES, CHAN), F32), vm((8, CHAN), F32), vm((7, 8, CHAN), F32),
            vm((MODES, CHAN), F32), vm((MODES, CHAN), F32),
            dma((6,)), dma, dma((NX,)), dma((NX,)), dma((NZ,)), dma, dma((10,)), dma((NY,)), dma((NY,)), dma, dma((4,)),
            dma((3,)), dma((3,)), dma((8,)), dma((8,)),
        ],
        compiler_params=pltpu.CompilerParams(
            collective_id=0, has_side_effects=True, vmem_limit_bytes=56 << 20
        ),
        cost_estimate=pl.CostEstimate(flops=2 * ROWS * 8192 * CHAN, bytes_accessed=4 << 20, transcendentals=0),
        name="hyena",
    )(query_stream, key_stream, value_stream, decay_rate.T, residue.T, skip_gain[None], out_weight)


def solution(mesh):
    placed = (
        P("seq", "tp"),
        P("seq", "tp"),
        P("seq", "tp"),
        P("tp", None),
        P("tp", None),
        P("tp"),
        P("seq", "tp"),
    )
    return jax.shard_map(
        body, mesh=mesh, in_specs=placed, out_specs=P("seq", "tp"), check_vma=False
    )
```

```python
import functools

import jax
import jax.numpy as jnp
from jax import lax
from jax.experimental import pallas as pl
from jax.experimental.pallas import tpu as pltpu
from jax.sharding import PartitionSpec as P

MESH = pl.DeviceIdType.MESH
F32, BF16 = jnp.float32, jnp.bfloat16

ROWS, CHAN, KROWS, MODES = 256, 1024, 512, 16
SEG = ROWS // 8
LANES = 128
GROUPS = CHAN // LANES

PIECES = (64, 64, 64, 64, 64, 32, 32, 64, 64)
STARTS = tuple(sum(PIECES[:p]) for p in range(len(PIECES)))
NP, ZFIRST, HALF_P = len(PIECES), 6, 4
UNIT = 64

EARLY = 2
Z_STATES = 3
Z_EARLY = 5

OWN = [(0, 0, p) for p in range(NP)]
X_RIGHT = (
    OWN
    + [(0, 1, 0), (0, 1, 1), (0, 1, 2), (-1, 0, 6)]
    + [(0, 1, 3), (0, 1, 4), (0, 1, 5)]
    + [(-1, 0, p) for p in (0, 2, 4, 5)]
    + [(-1, 1, p) for p in (0, 2, 5)]
)
X_LEFT = (
    OWN
    + [(0, 1, 0), (0, 1, 1), (0, 1, 2), (1, 0, 7), (1, 0, 8)]
    + [(0, 1, 3), (0, 1, 4), (0, 1, 5)]
    + [(1, 0, p) for p in (1, 3)]
    + [(1, 1, p) for p in (1, 3, 4)]
)
Z_SEND = (
    OWN[:Z_EARLY]
    + [None] * 4
    + OWN[Z_EARLY:]
    + [(dx, 0, p) for dx in (-1, 1, 2) for p in (6, 7, 8)]
)


def times(items):
    total, out = 0.0, []
    for item in items:
        total += 1.0 if item is None else PIECES[item[2]] / UNIT
        out.append(total)
    return out


GP = 256
Y_RIGHT = [(0, 0, p) for p in range(4)] + [(0, 1, p) for p in range(4)] + [(-1, 0, 0), (-1, 0, 2), (-1, 1, 0), (-1, 1, 2)]
Y_LEFT = [(0, 0, p) for p in range(4)] + [(0, 1, p) for p in range(4)] + [(1, 0, 1), (1, 0, 3), (1, 1, 1), (1, 1, 3)]
NY = len(Y_RIGHT)
Y_AT = 5.3


def expm1(u):
    series = jnp.ones_like(u)
    for n in range(8, 1, -1):
        series = 1.0 + series * u * (1.0 / n)
    return jnp.where(u > -0.3, u * series, jnp.exp(u) - 1.0)


def kernel(q_hbm, k_hbm, v_hbm, rate_hbm, res_hbm, skip_hbm, w_hbm, out_ref,
           q, k, v, rate, res, skip, wbuf, gbuf, acc, prod, conv, lam_b, coef_b, starts,
           e_own, e_sib, e_chip, e_in, e_zh, a_own, a_zh, s_in, lam_block,
           in_sem, own_sem, r_xr, r_xl, r_z, s_w, r_w, r_yr, r_yl, s_g, r_g,
           s_e, r_e, s_st, r_st):
    s, t = lax.axis_index("seq"), lax.axis_index("tp")
    x, zh, c = s // 4, (s // 2) % 2, s % 2
    zl, y = t // 4, t % 4

    def at(dx=0, dzh=0, dc=0, dy=0, dzl=0):
        x2, zh2, c2 = (x + dx + 4) % 4, (zh + dzh) % 2, (c + dc) % 2
        return ((x2 * 2 + zh2) * 2 + c2, ((zl + dzl) % 2) * 4 + (y + dy + 4) % 4)

    def chip_block(dx, dz):
        return ((x + dx + 4) % 4) * 2 + (zh + dz) % 2

    def remote(src, dst, ssem, rsem, device):
        return pltpu.make_async_remote_copy(
            src_ref=src, dst_ref=dst, send_sem=ssem, recv_sem=rsem, device_id=device, device_id_type=MESH
        )

    ins = [
        pltpu.make_async_copy(a, b, in_sem.at[i])
        for i, (a, b) in enumerate(
            ((k_hbm, k), (v_hbm, v), (rate_hbm, rate), (res_hbm, res), (skip_hbm, skip), (q_hbm, q))
        )
    ]
    for cp in ins:
        cp.start()
    partners = [at(dc=1), at(dy=1), at(dy=3), at(dzl=1)] + [
        at(dx=1), at(dx=2), at(dx=3), at(dzh=1)
    ]
    barrier = pltpu.get_barrier_semaphore()
    for device in partners:
        pl.semaphore_signal(barrier, inc=1, device_id=device, device_id_type=MESH)

    pl.semaphore_wait(barrier, len(partners))

    rows_out = [0]
    gated_out = [0]
    sent = []

    def start(copy):
        copy.start()
        sent.append(copy)

    have = {(0, 0, p) for p in range(NP)}

    def rows_of(p):
        return pl.ds(STARTS[p], PIECES[p])

    def piece(item):
        dx, dz, p = item
        return wbuf.at[chip_block(dx, dz) * 2 + c, rows_of(p)]

    def source(item):
        return w_hbm.at[rows_of(item[2])] if item[:2] == (0, 0) else piece(item)

    links = (
        (X_RIGHT, r_xr, dict(dx=1), -1, 0),
        (X_LEFT, r_xl, dict(dx=3), 1, 0),
        (Z_SEND, r_z, dict(dzh=1), 0, 1),
    )
    issued = [0] * len(links)
    limits = [EARLY, EARLY, EARLY]

    def issue():
        for i, (items, rsem, where, _, _) in enumerate(links):
            while issued[i] < min(limits[i], len(items)):
                r = issued[i]
                if items[r] is not None:
                    dx, dz, p = items[r]
                    if (dx % 4, dz, p) not in have:
                        break
                    remote(source(items[r]), piece(items[r]), s_w, rsem.at[r], at(**where)).start()
                    rows_out[0] += PIECES[p]
                issued[i] += 1

    def absorb(i, r):
        items, rsem, where, ox, oz = links[i]
        dx, dz, p = items[r]
        item = ((dx + ox) % 4, (dz + oz) % 2, p)
        assert item not in have and r < issued[i]
        have.add(item)
        ref = piece(item)
        remote(ref, ref, s_w, rsem.at[r], at(**where)).wait_recv()
        remote(ref, ref, s_w, r_w.at[group(item)], at(dc=1)).start()
        rows_out[0] += PIECES[p]
        issue()

    events = sorted(
        (time, i, r)
        for i, link in enumerate(links)
        for r, time in enumerate(times(link[0]))
        if link[0][r] is not None
    )
    events += [(Y_AT + r + 1.0, 3, r) for r in range(NY)]
    events += [(Z_EARLY + 2.0 + p, 4, p) for p in range(4)]
    events.sort()

    def absorb_until(time):
        while events and events[0][0] <= time and events[0][1] < 3:
            absorb(*events.pop(0)[1:])

    def group(item):
        dx, dz, p = item
        return dx * 2 + dz + (4 if (dx, dz) == (2, 1) and p >= HALF_P else 0)

    def from_sibling(dx, dz, part=None):
        rows = KROWS if part is None else KROWS // 2
        first = (part or 0) * rows
        ref = wbuf.at[chip_block(dx, dz) * 2 + 1 - c, pl.ds(first, rows)]
        remote(ref, ref, s_w, r_w.at[group((dx, dz, (part or 0) * HALF_P))], at(dc=1)).wait_recv()

    issue()
    own = wbuf.at[s]
    own_in = pltpu.make_async_copy(w_hbm, own, own_sem)
    own_in.start()
    start(remote(w_hbm, own, s_e.at[1], r_e.at[1], at(dc=1)))

    for cp in ins:
        cp.wait()
    rate_t, res_t = rate[...], res[...]
    lam_t = jnp.exp(-rate_t)
    coef_t = res_t * jnp.sqrt(-expm1(-2.0 * rate_t))
    for m in range(MODES):
        lam_b[m] = jnp.broadcast_to(lam_t[m : m + 1, :], (8, CHAN))
        coef_b[m] = jnp.broadcast_to(coef_t[m : m + 1, :], (8, CHAN))
    lam_block[...] = jnp.exp(-float(ROWS) * rate_t)

    for g in range(GROUPS):
        lanes = pl.ds(g * LANES, LANES)
        prod[g] = (k[:, lanes].astype(F32) * v[:, lanes].astype(F32)).astype(BF16).astype(F32)
    seg_at = lax.broadcasted_iota(jnp.int32, (MODES, 8, LANES), 1)
    for g in range(GROUPS):
        lanes = pl.ds(g * LANES, LANES)
        lam = lam_b[:, :, lanes]

        def ends(i, state):
            return lam * state + prod[g, pl.ds(i, 8, stride=SEG), :][None]

        state = lax.fori_loop(0, SEG, ends, jnp.zeros((MODES, 8, LANES), F32), unroll=4)
        power = lam
        for _ in range(5):
            power = power * power
        scan = state
        for step in (1, 2, 4):
            moved = jnp.where(seg_at >= step, pltpu.roll(scan, step, 1), 0.0)
            scan = scan + power * moved
            power = power * power
        starts[:, :, lanes] = jnp.where(seg_at >= 1, pltpu.roll(scan, 1, 1), 0.0)
        for m in range(MODES):
            e_own[pl.ds(m, 1), lanes] = scan[m, 7:8, :]

    pass_e = remote(e_own, e_sib, s_e.at[0], r_e.at[0], at(dc=1))
    start(pass_e)
    pass_e.wait_recv()
    half = pl.ds(pl.multiple_of(8 * c, 8), 8)
    lam_h = lam_block[half, :]
    mine, other = e_own[half, :], e_sib[half, :]
    lam2 = lam_h * lam_h
    lam4 = lam2 * lam2
    e_chip[...] = jnp.where(c == 0, lam_h * mine + other, lam_h * other + mine)
    later = []
    for d in range(1, 4):
        later.append((x + d < 4, remote(e_chip, e_in.at[x], s_st.at[d - 1], r_st.at[x], at(dx=d))))
    for ok, copy in later:
        pl.when(ok)(copy.start)
    start(remote(e_chip, e_zh, s_st.at[3], r_st.at[3], at(dzh=1)))
    limits[:] = [len(X_RIGHT), len(X_LEFT), Z_STATES]
    issue()
    absorb_until(2.0)
    a_own[...] = jnp.zeros((8, CHAN), F32)
    for x1 in range(3):

        @pl.when(x1 < x)
        def _(x1=x1):
            remote(e_chip, e_in.at[x1], s_st.at[0], r_st.at[x1], at(dx=1)).wait_recv()
            a_own[...] = lam4 * a_own[...] + e_in[x1]

    pass_a = remote(a_own, a_zh, s_st.at[4], r_st.at[4], at(dzh=1))
    start(pass_a)
    limits[2] = Z_EARLY
    issue()
    absorb_until(3.0)
    remote(e_chip, e_zh, s_st.at[3], r_st.at[3], at(dzh=1)).wait_recv()
    pass_a.wait_recv()
    s_x = jnp.where(zh == 0, lam2 * a_own[...] + a_zh[...], lam2 * a_zh[...] + a_own[...])
    s_half = s_in.at[half, :]
    s_half[...] = jnp.where(zh == 0, s_x, lam2 * s_x + e_zh[...])
    start(remote(s_half, s_half, s_e.at[2], r_e.at[2], at(dc=1)))
    absorb_until(4.0)
    pass_s_in = s_in.at[pl.ds(pl.multiple_of(8 - 8 * c, 8), 8), :]
    remote(pass_s_in, pass_s_in, s_e.at[2], r_e.at[2], at(dc=1)).wait_recv()

    have_g = set()

    def g_piece(item):
        dy, dz, p = item
        return gbuf.at[((zl + dz) % 2) * 4 + (y + dy + 4) % 4, :, pl.ds(p * GP, GP)]

    g_links = ((Y_RIGHT, r_yr, dict(dy=1), -1), (Y_LEFT, r_yl, dict(dy=3), 1))

    issued_g = [0] * len(g_links)

    def issue_g():
        for i, (items, rsem, where, _) in enumerate(g_links):
            while issued_g[i] < NY:
                r = issued_g[i]
                dy, dz, p = items[r]
                if (dy % 4, dz, p) not in have_g:
                    break
                ref = g_piece(items[r])
                remote(ref, ref, s_g, rsem.at[r], at(**where)).start()
                gated_out[0] += 1
                issued_g[i] += 1

    def absorb_zl(p):
        ref = g_piece((0, 1, p))
        remote(ref, ref, s_g, r_g.at[p], at(dzl=1)).wait_recv()
        have_g.add((0, 1, p))
        issue_g()

    def absorb_g(r):
        if r >= NY:
            return
        for items, rsem, where, oy in g_links:
            dy, dz, p = items[r]
            item = ((dy + oy) % 4, dz, p)
            ref = g_piece(item)
            remote(ref, ref, s_g, rsem.at[r], at(**where)).wait_recv()
            assert item not in have_g
            have_g.add(item)
        issue_g()

    before = jnp.where(c == 0, s_in[...], lam_block[...] * s_in[...] + e_sib[...])
    e_own_state = before
    row_seg = lax.broadcasted_iota(jnp.int32, (8, LANES), 0).astype(F32)
    for g in range(GROUPS):
        lanes = pl.ds(g * LANES, LANES)
        lam, coef = lam_b[:, :, lanes], coef_b[:, :, lanes]
        power = lam
        for _ in range(5):
            power = power * power
        lift = jnp.where(seg_at % 2 == 1, power, 1.0)
        power = power * power
        lift = lift * jnp.where((seg_at // 2) % 2 == 1, power, 1.0)
        power = power * power
        lift = lift * jnp.where(seg_at // 4 == 1, power, 1.0)
        first = jnp.stack([jnp.broadcast_to(e_own_state[m : m + 1, g * LANES : (g + 1) * LANES], (8, LANES)) for m in range(MODES)])
        gain = skip[:, lanes]

        def step(i, state):
            p = prod[g, pl.ds(i, 8, stride=SEG), :]
            state = lam * state + p[None]
            conv[g, pl.ds(i, 8, stride=SEG), :] = jnp.sum(coef * state, axis=0) + gain * p
            return state

        lax.fori_loop(0, SEG, step, starts[:, :, lanes] + lift * first, unroll=4)
        rounded = conv[g].astype(BF16).astype(F32)
        gbuf[t, :, lanes] = (q[:, lanes].astype(F32) * rounded).astype(BF16)
        if g % 2 == 1:
            p = g // 2
            have_g.add((0, 0, p))
            ref = g_piece((0, 0, p))
            remote(ref, ref, s_g, r_g.at[p], at(dzl=1)).start()
            gated_out[0] += 1
            issue_g()
            absorb_until(4.0 + 0.3 * p)

    limits[2] = len(Z_SEND)
    issue()

    def multiply(dx, dz, part=None, first=False, last=False):
        b = chip_block(dx, dz)
        rows = KROWS if part is None else KROWS // 2
        at_row = (part or 0) * rows

        for n in range(0, CHAN, 256):
            cols = pl.ds(n, 256)
            if part is None:
                w = wbuf[pl.ds(2 * b, 2), :, cols].reshape(2 * KROWS, 256)
                total = jnp.dot(gbuf[b], w, preferred_element_type=F32)
            else:
                total = sum(
                    jnp.dot(
                        gbuf[b, :, pl.ds(h * KROWS + at_row, rows)],
                        wbuf[2 * b + h, pl.ds(at_row, rows), cols],
                        preferred_element_type=F32,
                    )
                    for h in range(2)
                )
            total = total if first else acc[:, cols] + total
            if last:
                out_ref[:, cols] = total.astype(BF16)
            else:
                acc[:, cols] = total

    done = set()
    blocks = [(0, 0), (1, 0), (3, 0), (0, 1), (1, 1), (3, 1), (2, 0)]

    def work(most):
        for b in [b for b in blocks if b not in done and all((*b, p) in have for p in range(NP))][:most]:
            if b != (0, 0):
                from_sibling(*b)
            multiply(*b, first=not done)
            done.add(b)

    waits = [NY + 4]
    while events:
        _, i, r = events.pop(0)
        if i < 3:
            absorb(i, r)
        elif i == 3:
            absorb_g(r)
        else:
            absorb_zl(r)
        if i >= 3:
            waits[0] -= 1
            if not waits[0]:
                own_in.wait()
                remote(w_hbm, wbuf.at[s + 1 - 2 * c], s_e.at[1], r_e.at[1], at(dc=1)).wait_recv()
        if not waits[0] and len(events) > 1:
            work(1)
    work(8)
    assert len(done) == 7
    for part in range(2):
        from_sibling(2, 1, part)
        multiply(2, 1, part, last=part == 1)

    for copy in sent:
        copy.wait_send()
    assert rows_out[0] % KROWS == 0 and gated_out[0] % 4 == 0
    ref = wbuf.at[pl.ds(0, rows_out[0] // KROWS)]
    remote(ref, ref, s_w, r_w.at[0], at(dc=1)).wait_send()
    ref = gbuf.at[pl.ds(0, gated_out[0] // 4)]
    remote(ref, ref, s_g, r_g.at[0], at(dc=1)).wait_send()
    for ok, copy in later:
        pl.when(ok)(copy.wait_send)


def body(query_stream, key_stream, value_stream, decay_rate, residue, skip_gain, out_weight):
    dma = pltpu.SemaphoreType.DMA
    vm = pltpu.VMEM
    return pl.pallas_call(
        kernel,
        out_shape=pltpu.VMEM((ROWS, CHAN), BF16),
        in_specs=[pl.BlockSpec(memory_space=pl.ANY)] * 7,
        out_specs=pl.BlockSpec(memory_space=pltpu.VMEM),
        scratch_shapes=[
            vm((ROWS, CHAN), BF16), vm((ROWS, CHAN), BF16), vm((ROWS, CHAN), BF16),
            vm((MODES, CHAN), F32), vm((MODES, CHAN), F32), vm((1, CHAN), F32),
            vm((16, KROWS, CHAN), BF16), vm((8, ROWS, CHAN), BF16), vm((ROWS, CHAN), F32),
            vm((GROUPS, ROWS, LANES), F32), vm((GROUPS, ROWS, LANES), F32),
            vm((MODES, 8, CHAN), F32), vm((MODES, 8, CHAN), F32), vm((MODES, 8, CHAN), F32),
            vm((MODES, CHAN), F32), vm((MODES, CHAN), F32), vm((8, CHAN), F32), vm((3, 8, CHAN), F32),
            vm((8, CHAN), F32), vm((8, CHAN), F32), vm((8, CHAN), F32),
            vm((MODES, CHAN), F32), vm((MODES, CHAN), F32),
            dma((6,)), dma, dma((len(X_RIGHT),)), dma((len(X_LEFT),)), dma((len(Z_SEND),)), dma, dma((10,)), dma((NY,)), dma((NY,)), dma, dma((4,)),
            dma((3,)), dma((3,)), dma((5,)), dma((5,)),
        ],
        compiler_params=pltpu.CompilerParams(
            collective_id=0, has_side_effects=True, vmem_limit_bytes=56 << 20
        ),
        cost_estimate=pl.CostEstimate(flops=2 * ROWS * 8192 * CHAN, bytes_accessed=4 << 20, transcendentals=0),
        name="hyena",
    )(query_stream, key_stream, value_stream, decay_rate.T, residue.T, skip_gain[None], out_weight)


def solution(mesh):
    placed = (
        P("seq", "tp"),
        P("seq", "tp"),
        P("seq", "tp"),
        P("tp", None),
        P("tp", None),
        P("tp"),
        P("seq", "tp"),
    )
    return jax.shard_map(
        body, mesh=mesh, in_specs=placed, out_specs=P("seq", "tp"), check_vma=False
    )
```

```python
import functools

import jax
import jax.numpy as jnp
from jax import lax
from jax.experimental import pallas as pl
from jax.experimental.pallas import tpu as pltpu
from jax.sharding import PartitionSpec as P

MESH = pl.DeviceIdType.MESH
F32, BF16 = jnp.float32, jnp.bfloat16

ROWS, CHAN, KROWS, MODES = 256, 1024, 512, 16
SEG = ROWS // 8
LANES = 128
GROUPS = CHAN // LANES

GRAIN = 16
UNIT = 64

EARLY = 2
Z_STATES = 3
Z_EARLY = 4

X_OWN = [(0, 0, 0, 64), (0, 0, 64, 64), (0, 0, 128, 128), (0, 0, 256, 96), (0, 0, 352, 160)]
X_RIGHT = X_OWN + [
    (0, 1, 0, 128), (0, 1, 128, 64), (-1, 0, 352, 48), (0, 1, 192, 160),
    (-1, 0, 0, 128), (-1, 0, 128, 96),
    (-1, 1, 0, 96), (-1, 1, 256, 64),
]
X_LEFT = X_OWN + [
    (0, 1, 0, 128), (0, 1, 128, 64), (1, 0, 400, 112), (0, 1, 192, 160),
    (1, 0, 224, 128),
    (1, 1, 96, 160), (1, 1, 320, 32),
]
Z_SEND = [(0, 0, 0, 64), (0, 0, 64, 64), (0, 0, 128, 64), (0, 0, 192, 160)] + [None] * 4 + [
    (0, 0, 352, 160), (-1, 0, 352, 160), (1, 0, 352, 160), (2, 0, 352, 48), (2, 0, 400, 112),
]


def times(items):
    total, out = 0.0, []
    for item in items:
        total += 1.0 if item is None else item[3] / UNIT
        out.append(total)
    return out


def grains(dx, dz, first, rows):
    return {(dx % 4, dz % 2, g) for g in range(first // GRAIN, (first + rows) // GRAIN)}


GP = 256
Y_RIGHT = [(0, 0, p) for p in range(4)] + [(-1, 0, 0), (-1, 0, 2)] + [(0, 1, p) for p in range(4)] + [(-1, 1, 0), (-1, 1, 2)]
Y_LEFT = [(0, 0, p) for p in range(4)] + [(1, 0, 1), (1, 0, 3)] + [(0, 1, p) for p in range(4)] + [(1, 1, 1), (1, 1, 3)]
NY = len(Y_RIGHT)
Y_AT = 5.3


def expm1(u):
    series = jnp.ones_like(u)
    for n in range(8, 1, -1):
        series = 1.0 + series * u * (1.0 / n)
    return jnp.where(u > -0.3, u * series, jnp.exp(u) - 1.0)


def kernel(q_hbm, k_hbm, v_hbm, rate_hbm, res_hbm, skip_hbm, w_hbm, out_ref,
           q, k, v, rate, res, skip, wbuf, gbuf, acc, prod, conv, lam_b, coef_b, starts,
           e_own, e_sib, e_chip, e_in, e_zh, a_own, a_zh, s_in, lam_block,
           in_sem, own_sem, r_xr, r_xl, r_z, s_w, r_w, r_yr, r_yl, s_g, r_g,
           s_e, r_e, s_st, r_st):
    s, t = lax.axis_index("seq"), lax.axis_index("tp")
    x, zh, c = s // 4, (s // 2) % 2, s % 2
    zl, y = t // 4, t % 4

    def at(dx=0, dzh=0, dc=0, dy=0, dzl=0):
        x2, zh2, c2 = (x + dx + 4) % 4, (zh + dzh) % 2, (c + dc) % 2
        return ((x2 * 2 + zh2) * 2 + c2, ((zl + dzl) % 2) * 4 + (y + dy + 4) % 4)

    def chip_block(dx, dz):
        return ((x + dx + 4) % 4) * 2 + (zh + dz) % 2

    def remote(src, dst, ssem, rsem, device):
        return pltpu.make_async_remote_copy(
            src_ref=src, dst_ref=dst, send_sem=ssem, recv_sem=rsem, device_id=device, device_id_type=MESH
        )

    ins = [
        pltpu.make_async_copy(a, b, in_sem.at[i])
        for i, (a, b) in enumerate(
            ((k_hbm, k), (v_hbm, v), (rate_hbm, rate), (res_hbm, res), (skip_hbm, skip), (q_hbm, q))
        )
    ]
    for cp in ins:
        cp.start()
    partners = [
        at(dzh=1), at(dx=2), at(dx=1), at(dx=3), at(dy=1), at(dy=3), at(dzl=1), at(dc=1)
    ]
    barrier = pltpu.get_barrier_semaphore()
    for device in partners:
        pl.semaphore_signal(barrier, inc=1, device_id=device, device_id_type=MESH)

    pl.semaphore_wait(barrier, len(partners))

    rows_out = [0]
    gated_out = [0]
    sent = []

    def start(copy):
        copy.start()
        sent.append(copy)

    have = grains(0, 0, 0, KROWS)

    def piece(item):
        dx, dz, first, rows = item
        return wbuf.at[chip_block(dx, dz) * 2 + c, pl.ds(first, rows)]

    def source(item):
        return w_hbm.at[pl.ds(item[2], item[3])] if item[:2] == (0, 0) else piece(item)

    links = (
        (X_RIGHT, r_xr, dict(dx=1), -1, 0),
        (X_LEFT, r_xl, dict(dx=3), 1, 0),
        (Z_SEND, r_z, dict(dzh=1), 0, 1),
    )
    issued = [0] * len(links)
    limits = [EARLY, EARLY, EARLY]

    def issue():
        for i, (items, rsem, where, _, _) in enumerate(links):
            while issued[i] < min(limits[i], len(items)):
                r = issued[i]
                if items[r] is not None:
                    if not grains(*items[r]) <= have:
                        break
                    remote(source(items[r]), piece(items[r]), s_w, rsem.at[r], at(**where)).start()
                    rows_out[0] += items[r][3]
                issued[i] += 1

    def absorb(i, r):
        items, rsem, where, ox, oz = links[i]
        dx, dz, first, rows = items[r]
        item = ((dx + ox) % 4, (dz + oz) % 2, first, rows)
        assert not grains(*item) & have and r < issued[i]
        have.update(grains(*item))
        ref = piece(item)
        remote(ref, ref, s_w, rsem.at[r], at(**where)).wait_recv()
        remote(ref, ref, s_w, r_w.at[group(item)], at(dc=1)).start()
        rows_out[0] += rows
        issue()

    events = sorted(
        (time + (i == 2) * 0.5, i, r)
        for i, link in enumerate(links)
        for r, time in enumerate(times(link[0]))
        if link[0][r] is not None
    )
    events += [(Y_AT + r + 1.0, 3, r) for r in range(NY)]
    events += [(times(Z_SEND)[Z_EARLY + p] + 1.0, 4, p) for p in range(4)]
    events.sort()

    def absorb_until(time):
        while events and events[0][0] <= time and events[0][1] < 3:
            absorb(*events.pop(0)[1:])

    def group(item):
        dx, dz, first, rows = item
        if (dx, dz) != (2, 1):
            return dx * 2 + dz
        assert first >= KROWS // 2 or first + rows <= KROWS // 2
        return 8 + first // (KROWS // 2)

    def from_sibling(dx, dz, part=None):
        rows = KROWS if part is None else KROWS // 2
        first = (part or 0) * rows
        ref = wbuf.at[chip_block(dx, dz) * 2 + 1 - c, pl.ds(first, rows)]
        remote(ref, ref, s_w, r_w.at[group((dx, dz, first, rows))], at(dc=1)).wait_recv()

    issue()
    own = wbuf.at[s]
    own_in = pltpu.make_async_copy(w_hbm, own, own_sem)
    own_in.start()
    start(remote(w_hbm, own, s_e.at[1], r_e.at[1], at(dc=1)))

    for cp in ins:
        cp.wait()
    rate_t, res_t = rate[...], res[...]
    lam_t = jnp.exp(-rate_t)
    coef_t = res_t * jnp.sqrt(-expm1(-2.0 * rate_t))
    for m in range(MODES):
        lam_b[m] = jnp.broadcast_to(lam_t[m : m + 1, :], (8, CHAN))
        coef_b[m] = jnp.broadcast_to(coef_t[m : m + 1, :], (8, CHAN))
    lam_block[...] = jnp.exp(-float(ROWS) * rate_t)

    for g in range(GROUPS):
        lanes = pl.ds(g * LANES, LANES)
        prod[g] = (k[:, lanes].astype(F32) * v[:, lanes].astype(F32)).astype(BF16).astype(F32)
    seg_at = lax.broadcasted_iota(jnp.int32, (MODES, 8, LANES), 1)
    for g in range(GROUPS):
        lanes = pl.ds(g * LANES, LANES)
        lam = lam_b[:, :, lanes]

        def ends(i, state):
            return lam * state + prod[g, pl.ds(i, 8, stride=SEG), :][None]

        state = lax.fori_loop(0, SEG, ends, jnp.zeros((MODES, 8, LANES), F32), unroll=4)
        power = lam
        for _ in range(5):
            power = power * power
        scan = state
        for step in (1, 2, 4):
            moved = jnp.where(seg_at >= step, pltpu.roll(scan, step, 1), 0.0)
            scan = scan + power * moved
            power = power * power
        starts[:, :, lanes] = jnp.where(seg_at >= 1, pltpu.roll(scan, 1, 1), 0.0)
        for m in range(MODES):
            e_own[pl.ds(m, 1), lanes] = scan[m, 7:8, :]

    pass_e = remote(e_own, e_sib, s_e.at[0], r_e.at[0], at(dc=1))
    start(pass_e)
    pass_e.wait_recv()
    half = pl.ds(pl.multiple_of(8 * c, 8), 8)
    lam_h = lam_block[half, :]
    mine, other = e_own[half, :], e_sib[half, :]
    lam2 = lam_h * lam_h
    lam4 = lam2 * lam2
    e_chip[...] = jnp.where(c == 0, lam_h * mine + other, lam_h * other + mine)
    later = []
    for d in range(1, 4):
        later.append((x + d < 4, remote(e_chip, e_in.at[x], s_st.at[d - 1], r_st.at[x], at(dx=d))))
    for ok, copy in later:
        pl.when(ok)(copy.start)
    start(remote(e_chip, e_zh, s_st.at[3], r_st.at[3], at(dzh=1)))
    limits[:] = [len(X_RIGHT), len(X_LEFT), Z_STATES]
    issue()
    absorb_until(2.0)
    a_own[...] = jnp.zeros((8, CHAN), F32)
    for x1 in range(3):

        @pl.when(x1 < x)
        def _(x1=x1):
            remote(e_chip, e_in.at[x1], s_st.at[0], r_st.at[x1], at(dx=1)).wait_recv()
            a_own[...] = lam4 * a_own[...] + e_in[x1]

    pass_a = remote(a_own, a_zh, s_st.at[4], r_st.at[4], at(dzh=1))
    start(pass_a)
    limits[2] = Z_EARLY
    issue()
    absorb_until(3.0)
    remote(e_chip, e_zh, s_st.at[3], r_st.at[3], at(dzh=1)).wait_recv()
    pass_a.wait_recv()
    s_x = jnp.where(zh == 0, lam2 * a_own[...] + a_zh[...], lam2 * a_zh[...] + a_own[...])
    s_half = s_in.at[half, :]
    s_half[...] = jnp.where(zh == 0, s_x, lam2 * s_x + e_zh[...])
    start(remote(s_half, s_half, s_e.at[2], r_e.at[2], at(dc=1)))
    absorb_until(4.0)
    pass_s_in = s_in.at[pl.ds(pl.multiple_of(8 - 8 * c, 8), 8), :]
    remote(pass_s_in, pass_s_in, s_e.at[2], r_e.at[2], at(dc=1)).wait_recv()

    have_g = set()

    def g_piece(item):
        dy, dz, p = item
        return gbuf.at[((zl + dz) % 2) * 4 + (y + dy + 4) % 4, :, pl.ds(p * GP, GP)]

    g_links = ((Y_RIGHT, r_yr, dict(dy=1), -1), (Y_LEFT, r_yl, dict(dy=3), 1))

    issued_g = [0] * len(g_links)

    def issue_g():
        for i, (items, rsem, where, _) in enumerate(g_links):
            while issued_g[i] < NY:
                r = issued_g[i]
                dy, dz, p = items[r]
                if (dy % 4, dz, p) not in have_g:
                    break
                ref = g_piece(items[r])
                remote(ref, ref, s_g, rsem.at[r], at(**where)).start()
                gated_out[0] += 1
                issued_g[i] += 1

    def absorb_zl(p):
        ref = g_piece((0, 1, p))
        remote(ref, ref, s_g, r_g.at[p], at(dzl=1)).wait_recv()
        have_g.add((0, 1, p))
        issue_g()

    def absorb_g(r):
        if r >= NY:
            return
        for items, rsem, where, oy in g_links:
            dy, dz, p = items[r]
            item = ((dy + oy) % 4, dz, p)
            ref = g_piece(item)
            remote(ref, ref, s_g, rsem.at[r], at(**where)).wait_recv()
            assert item not in have_g
            have_g.add(item)
        issue_g()

    before = jnp.where(c == 0, s_in[...], lam_block[...] * s_in[...] + e_sib[...])
    row_seg = lax.broadcasted_iota(jnp.int32, (8, LANES), 0).astype(F32)
    for g in range(GROUPS):
        lanes = pl.ds(g * LANES, LANES)
        lam, coef = lam_b[:, :, lanes], coef_b[:, :, lanes]
        power = lam
        for _ in range(5):
            power = power * power
        lift = jnp.where(seg_at % 2 == 1, power, 1.0)
        power = power * power
        lift = lift * jnp.where((seg_at // 2) % 2 == 1, power, 1.0)
        power = power * power
        lift = lift * jnp.where(seg_at // 4 == 1, power, 1.0)
        first = jnp.stack([jnp.broadcast_to(before[m : m + 1, g * LANES : (g + 1) * LANES], (8, LANES)) for m in range(MODES)])
        gain = skip[:, lanes]

        def step(i, state):
            p = prod[g, pl.ds(i, 8, stride=SEG), :]
            state = lam * state + p[None]
            conv[g, pl.ds(i, 8, stride=SEG), :] = jnp.sum(coef * state, axis=0) + gain * p
            return state

        lax.fori_loop(0, SEG, step, starts[:, :, lanes] + lift * first, unroll=4)
        rounded = conv[g].astype(BF16).astype(F32)
        gbuf[t, :, lanes] = (q[:, lanes].astype(F32) * rounded).astype(BF16)
        if g % 2 == 1:
            p = g // 2
            have_g.add((0, 0, p))
            ref = g_piece((0, 0, p))
            remote(ref, ref, s_g, r_g.at[p], at(dzl=1)).start()
            gated_out[0] += 1
            issue_g()
            absorb_until(4.0 + 0.3 * p)

    limits[2] = len(Z_SEND)
    issue()

    def multiply(dx, dz, part=None, first=False, last=False):
        b = chip_block(dx, dz)
        rows = KROWS if part is None else KROWS // 2
        at_row = (part or 0) * rows

        for n in range(0, CHAN, 256):
            cols = pl.ds(n, 256)
            if part is None:
                w = wbuf[pl.ds(2 * b, 2), :, cols].reshape(2 * KROWS, 256)
                total = jnp.dot(gbuf[b], w, preferred_element_type=F32)
            else:
                total = sum(
                    jnp.dot(
                        gbuf[b, :, pl.ds(h * KROWS + at_row, rows)],
                        wbuf[2 * b + h, pl.ds(at_row, rows), cols],
                        preferred_element_type=F32,
                    )
                    for h in range(2)
                )
            total = total if first else acc[:, cols] + total
            if last:
                out_ref[:, cols] = total.astype(BF16)
            else:
                acc[:, cols] = total

    done = set()
    blocks = [(0, 0), (1, 0), (3, 0), (0, 1), (1, 1), (3, 1), (2, 0)]

    def work(most):
        for b in [b for b in blocks if b not in done and grains(*b, 0, KROWS) <= have][:most]:
            if b != (0, 0):
                from_sibling(*b)
            multiply(*b, first=not done)
            done.add(b)

    waits = [NY + 4]
    while events:
        _, i, r = events.pop(0)
        if i < 3:
            absorb(i, r)
        elif i == 3:
            absorb_g(r)
        else:
            absorb_zl(r)
        if i >= 3:
            waits[0] -= 1
            if not waits[0]:
                own_in.wait()
                remote(w_hbm, wbuf.at[s + 1 - 2 * c], s_e.at[1], r_e.at[1], at(dc=1)).wait_recv()
        if not waits[0] and len(events) > 2:
            work(1)
    work(8)
    assert len(done) == 7
    for part in range(2):
        from_sibling(2, 1, part)
        multiply(2, 1, part, last=part == 1)

    for copy in sent:
        copy.wait_send()
    assert rows_out[0] % KROWS == 0 and gated_out[0] % 4 == 0
    ref = wbuf.at[pl.ds(0, rows_out[0] // KROWS)]
    remote(ref, ref, s_w, r_w.at[0], at(dc=1)).wait_send()
    ref = gbuf.at[pl.ds(0, gated_out[0] // 4)]
    remote(ref, ref, s_g, r_g.at[0], at(dc=1)).wait_send()
    for ok, copy in later:
        pl.when(ok)(copy.wait_send)


def body(query_stream, key_stream, value_stream, decay_rate, residue, skip_gain, out_weight):
    dma = pltpu.SemaphoreType.DMA
    vm = pltpu.VMEM
    return pl.pallas_call(
        kernel,
        out_shape=pltpu.VMEM((ROWS, CHAN), BF16),
        in_specs=[pl.BlockSpec(memory_space=pl.ANY)] * 7,
        out_specs=pl.BlockSpec(memory_space=pltpu.VMEM),
        scratch_shapes=[
            vm((ROWS, CHAN), BF16), vm((ROWS, CHAN), BF16), vm((ROWS, CHAN), BF16),
            vm((MODES, CHAN), F32), vm((MODES, CHAN), F32), vm((1, CHAN), F32),
            vm((16, KROWS, CHAN), BF16), vm((8, ROWS, CHAN), BF16), vm((ROWS, CHAN), F32),
            vm((GROUPS, ROWS, LANES), F32), vm((GROUPS, ROWS, LANES), F32),
            vm((MODES, 8, CHAN), F32), vm((MODES, 8, CHAN), F32), vm((MODES, 8, CHAN), F32),
            vm((MODES, CHAN), F32), vm((MODES, CHAN), F32), vm((8, CHAN), F32), vm((4, 8, CHAN), F32),
            vm((8, CHAN), F32), vm((8, CHAN), F32), vm((8, CHAN), F32),
            vm((MODES, CHAN), F32), vm((MODES, CHAN), F32),
            dma((6,)), dma, dma((len(X_RIGHT),)), dma((len(X_LEFT),)), dma((len(Z_SEND),)), dma, dma((10,)), dma((NY,)), dma((NY,)), dma, dma((4,)),
            dma((3,)), dma((3,)), dma((5,)), dma((5,)),
        ],
        compiler_params=pltpu.CompilerParams(
            collective_id=0, has_side_effects=True, vmem_limit_bytes=56 << 20
        ),
        cost_estimate=pl.CostEstimate(flops=2 * ROWS * 8192 * CHAN, bytes_accessed=4 << 20, transcendentals=0),
        name="hyena",
    )(query_stream, key_stream, value_stream, decay_rate.T, residue.T, skip_gain[None], out_weight)


def solution(mesh):
    placed = (
        P("seq", "tp"),
        P("seq", "tp"),
        P("seq", "tp"),
        P("tp", None),
        P("tp", None),
        P("tp"),
        P("seq", "tp"),
    )
    return jax.shard_map(
        body, mesh=mesh, in_specs=placed, out_specs=P("seq", "tp"), check_vma=False
    )
```

```python
import functools

import jax
import jax.numpy as jnp
from jax import lax
from jax.experimental import pallas as pl
from jax.experimental.pallas import tpu as pltpu
from jax.sharding import PartitionSpec as P

MESH = pl.DeviceIdType.MESH
F32, BF16 = jnp.float32, jnp.bfloat16

ROWS, CHAN, KROWS, MODES = 256, 1024, 512, 16
SEG = ROWS // 8
LANES = 128
GROUPS = CHAN // LANES

GRAIN = 16
UNIT = 64

EARLY = 2
Z_STATES = 3
Z_EARLY = 4

X_OWN = [(0, 0, 0, 64), (0, 0, 64, 64), (0, 0, 128, 128), (0, 0, 256, 96), (0, 0, 352, 160)]
X_RIGHT = X_OWN + [
    (0, 1, 0, 128), (0, 1, 128, 64), (-1, 0, 352, 48), (0, 1, 192, 160),
    (-1, 0, 0, 128), (-1, 0, 128, 96),
    (-1, 1, 0, 96), (-1, 1, 256, 64),
]
X_LEFT = X_OWN + [
    (0, 1, 0, 128), (0, 1, 128, 64), (1, 0, 400, 112), (0, 1, 192, 160),
    (1, 0, 224, 128),
    (1, 1, 96, 160), (1, 1, 320, 32),
]
Z_SEND = [(0, 0, 0, 64), (0, 0, 64, 64), (0, 0, 128, 64), (0, 0, 192, 160)] + [None] * 4 + [
    (0, 0, 352, 160), (-1, 0, 352, 160), (1, 0, 352, 160), (2, 0, 352, 48), (2, 0, 400, 112),
]


def times(items):
    total, out = 0.0, []
    for item in items:
        total += 1.0 if item is None else item[3] / UNIT
        out.append(total)
    return out


def grains(dx, dz, first, rows):
    return {(dx % 4, dz % 2, g) for g in range(first // GRAIN, (first + rows) // GRAIN)}


GP = 256
Y_RIGHT = [(0, 0, p) for p in range(4)] + [(-1, 0, 0), (-1, 0, 2)] + [(0, 1, p) for p in range(4)] + [(-1, 1, 0), (-1, 1, 2)]
Y_LEFT = [(0, 0, p) for p in range(4)] + [(1, 0, 1), (1, 0, 3)] + [(0, 1, p) for p in range(4)] + [(1, 1, 1), (1, 1, 3)]
NY = len(Y_RIGHT)
Y_AT = 5.3


def expm1(u):
    series = jnp.ones_like(u)
    for n in range(8, 1, -1):
        series = 1.0 + series * u * (1.0 / n)
    return jnp.where(u > -0.3, u * series, jnp.exp(u) - 1.0)


def kernel(q_hbm, k_hbm, v_hbm, rate_hbm, res_hbm, skip_hbm, w_hbm, out_ref,
           q, k, v, rate, res, skip, wbuf, gbuf, acc, prod, conv, lam_b, coef_b, starts,
           e_own, e_sib, e_chip, e_in, e_zh, a_own, a_zh, s_in, lam_block,
           in_sem, own_sem, r_xr, r_xl, r_z, s_w, r_w, r_yr, r_yl, s_g, r_g,
           s_e, r_e, s_st, r_st):
    s, t = lax.axis_index("seq"), lax.axis_index("tp")
    x, zh, c = s // 4, (s // 2) % 2, s % 2
    zl, y = t // 4, t % 4

    def at(dx=0, dzh=0, dc=0, dy=0, dzl=0):
        x2, zh2, c2 = (x + dx + 4) % 4, (zh + dzh) % 2, (c + dc) % 2
        return ((x2 * 2 + zh2) * 2 + c2, ((zl + dzl) % 2) * 4 + (y + dy + 4) % 4)

    def chip_block(dx, dz):
        return ((x + dx + 4) % 4) * 2 + (zh + dz) % 2

    def remote(src, dst, ssem, rsem, device):
        return pltpu.make_async_remote_copy(
            src_ref=src, dst_ref=dst, send_sem=ssem, recv_sem=rsem, device_id=device, device_id_type=MESH
        )

    ins = [
        pltpu.make_async_copy(a, b, in_sem.at[i])
        for i, (a, b) in enumerate(
            ((k_hbm, k), (v_hbm, v), (rate_hbm, rate), (res_hbm, res), (skip_hbm, skip), (q_hbm, q))
        )
    ]
    for cp in ins:
        cp.start()
    partners = [
        at(dzh=1), at(dx=2), at(dx=1), at(dx=3), at(dy=1), at(dy=3), at(dzl=1), at(dc=1)
    ]
    barrier = pltpu.get_barrier_semaphore()
    for device in partners:
        pl.semaphore_signal(barrier, inc=1, device_id=device, device_id_type=MESH)

    pl.semaphore_wait(barrier, len(partners))

    rows_out = [0]
    gated_out = [0]
    sent = []

    def start(copy):
        copy.start()
        sent.append(copy)

    have = grains(0, 0, 0, KROWS)

    def piece(item):
        dx, dz, first, rows = item
        return wbuf.at[chip_block(dx, dz) * 2 + c, pl.ds(first, rows)]

    def source(item):
        return w_hbm.at[pl.ds(item[2], item[3])] if item[:2] == (0, 0) else piece(item)

    links = (
        (X_RIGHT, r_xr, dict(dx=1), -1, 0),
        (X_LEFT, r_xl, dict(dx=3), 1, 0),
        (Z_SEND, r_z, dict(dzh=1), 0, 1),
    )
    issued = [0] * len(links)
    limits = [EARLY, EARLY, EARLY]

    def issue():
        for i, (items, rsem, where, _, _) in enumerate(links):
            while issued[i] < min(limits[i], len(items)):
                r = issued[i]
                if items[r] is not None:
                    if not grains(*items[r]) <= have:
                        break
                    remote(source(items[r]), piece(items[r]), s_w, rsem.at[r], at(**where)).start()
                    rows_out[0] += items[r][3]
                issued[i] += 1

    def absorb(i, r):
        items, rsem, where, ox, oz = links[i]
        dx, dz, first, rows = items[r]
        item = ((dx + ox) % 4, (dz + oz) % 2, first, rows)
        assert not grains(*item) & have and r < issued[i]
        have.update(grains(*item))
        ref = piece(item)
        remote(ref, ref, s_w, rsem.at[r], at(**where)).wait_recv()
        remote(ref, ref, s_w, r_w.at[group(item)], at(dc=1)).start()
        rows_out[0] += rows
        issue()

    events = sorted(
        (time + (i == 2) * 0.5, i, r)
        for i, link in enumerate(links)
        for r, time in enumerate(times(link[0]))
        if link[0][r] is not None
    )
    events += [(Y_AT + r + 1.0, 3, r) for r in range(NY)]
    events += [(times(Z_SEND)[Z_EARLY + p] + 1.0, 4, p) for p in range(4)]
    events.sort()

    def absorb_until(time):
        while events and events[0][0] <= time and events[0][1] < 3:
            absorb(*events.pop(0)[1:])

    def group(item):
        dx, dz, first, rows = item
        if (dx, dz) != (2, 1):
            return dx * 2 + dz
        assert first >= KROWS // 2 or first + rows <= KROWS // 2
        return 8 + first // (KROWS // 2)

    def from_sibling(dx, dz, part=None):
        rows = KROWS if part is None else KROWS // 2
        first = (part or 0) * rows
        ref = wbuf.at[chip_block(dx, dz) * 2 + 1 - c, pl.ds(first, rows)]
        remote(ref, ref, s_w, r_w.at[group((dx, dz, first, rows))], at(dc=1)).wait_recv()

    issue()
    own = wbuf.at[s]
    own_in = pltpu.make_async_copy(w_hbm, own, own_sem)
    own_in.start()
    start(remote(w_hbm, own, s_e.at[1], r_e.at[1], at(dc=1)))

    for cp in ins:
        cp.wait()
    rate_t, res_t = rate[...], res[...]
    lam_t = jnp.exp(-rate_t)
    coef_t = res_t * jnp.sqrt(-expm1(-2.0 * rate_t))
    for m in range(MODES):
        lam_b[m] = jnp.broadcast_to(lam_t[m : m + 1, :], (8, CHAN))
        coef_b[m] = jnp.broadcast_to(coef_t[m : m + 1, :], (8, CHAN))
    lam_block[...] = jnp.exp(-float(ROWS) * rate_t)

    for g in range(GROUPS):
        lanes = pl.ds(g * LANES, LANES)
        prod[g] = (k[:, lanes].astype(F32) * v[:, lanes].astype(F32)).astype(BF16).astype(F32)
    seg_at = lax.broadcasted_iota(jnp.int32, (MODES, 8, LANES), 1)
    for g in range(GROUPS):
        lanes = pl.ds(g * LANES, LANES)
        lam = lam_b[:, :, lanes]

        def ends(i, state):
            return lam * state + prod[g, pl.ds(i, 8, stride=SEG), :][None]

        state = lax.fori_loop(0, SEG, ends, jnp.zeros((MODES, 8, LANES), F32), unroll=4)
        power = lam
        for _ in range(5):
            power = power * power
        scan = state
        for step in (1, 2, 4):
            moved = jnp.where(seg_at >= step, pltpu.roll(scan, step, 1), 0.0)
            scan = scan + power * moved
            power = power * power
        starts[:, :, lanes] = jnp.where(seg_at >= 1, pltpu.roll(scan, 1, 1), 0.0)
        for m in range(MODES):
            e_own[pl.ds(m, 1), lanes] = scan[m, 7:8, :]

    pass_e = remote(e_own, e_sib, s_e.at[0], r_e.at[0], at(dc=1))
    start(pass_e)
    pass_e.wait_recv()
    half = pl.ds(pl.multiple_of(8 * c, 8), 8)
    lam_h = lam_block[half, :]
    mine, other = e_own[half, :], e_sib[half, :]
    lam2 = lam_h * lam_h
    lam4 = lam2 * lam2
    e_chip[...] = jnp.where(c == 0, lam_h * mine + other, lam_h * other + mine)
    later = []
    for d in range(1, 4):
        later.append((x + d < 4, remote(e_chip, e_in.at[x], s_st.at[d - 1], r_st.at[x], at(dx=d))))
    for ok, copy in later:
        pl.when(ok)(copy.start)
    start(remote(e_chip, e_zh, s_st.at[3], r_st.at[3], at(dzh=1)))
    limits[:] = [len(X_RIGHT), len(X_LEFT), Z_STATES]
    issue()
    absorb_until(2.0)
    a_own[...] = jnp.zeros((8, CHAN), F32)
    for x1 in range(3):

        @pl.when(x1 < x)
        def _(x1=x1):
            remote(e_chip, e_in.at[x1], s_st.at[0], r_st.at[x1], at(dx=1)).wait_recv()
            a_own[...] = lam4 * a_own[...] + e_in[x1]

    pass_a = remote(a_own, a_zh, s_st.at[4], r_st.at[4], at(dzh=1))
    start(pass_a)
    limits[2] = Z_EARLY
    issue()
    absorb_until(3.0)
    remote(e_chip, e_zh, s_st.at[3], r_st.at[3], at(dzh=1)).wait_recv()
    pass_a.wait_recv()
    s_x = jnp.where(zh == 0, lam2 * a_own[...] + a_zh[...], lam2 * a_zh[...] + a_own[...])
    s_half = s_in.at[half, :]
    s_half[...] = jnp.where(zh == 0, s_x, lam2 * s_x + e_zh[...])
    start(remote(s_half, s_half, s_e.at[2], r_e.at[2], at(dc=1)))
    absorb_until(4.0)
    pass_s_in = s_in.at[pl.ds(pl.multiple_of(8 - 8 * c, 8), 8), :]
    remote(pass_s_in, pass_s_in, s_e.at[2], r_e.at[2], at(dc=1)).wait_recv()

    have_g = set()

    def g_piece(item):
        dy, dz, p = item
        return gbuf.at[((zl + dz) % 2) * 4 + (y + dy + 4) % 4, :, pl.ds(p * GP, GP)]

    g_links = ((Y_RIGHT, r_yr, dict(dy=1), -1), (Y_LEFT, r_yl, dict(dy=3), 1))

    issued_g = [0] * len(g_links)

    def issue_g():
        for i, (items, rsem, where, _) in enumerate(g_links):
            while issued_g[i] < NY:
                r = issued_g[i]
                dy, dz, p = items[r]
                if (dy % 4, dz, p) not in have_g:
                    break
                ref = g_piece(items[r])
                remote(ref, ref, s_g, rsem.at[r], at(**where)).start()
                gated_out[0] += 1
                issued_g[i] += 1

    def absorb_zl(p):
        ref = g_piece((0, 1, p))
        remote(ref, ref, s_g, r_g.at[p], at(dzl=1)).wait_recv()
        have_g.add((0, 1, p))
        issue_g()

    def absorb_g(r):
        if r >= NY:
            return
        for items, rsem, where, oy in g_links:
            dy, dz, p = items[r]
            item = ((dy + oy) % 4, dz, p)
            ref = g_piece(item)
            remote(ref, ref, s_g, rsem.at[r], at(**where)).wait_recv()
            assert item not in have_g
            have_g.add(item)
        issue_g()

    before = jnp.where(c == 0, s_in[...], lam_block[...] * s_in[...] + e_sib[...])
    row_seg = lax.broadcasted_iota(jnp.int32, (8, LANES), 0).astype(F32)
    for g in range(GROUPS):
        lanes = pl.ds(g * LANES, LANES)
        lam, coef = lam_b[:, :, lanes], coef_b[:, :, lanes]
        power = lam
        for _ in range(5):
            power = power * power
        lift = jnp.where(seg_at % 2 == 1, power, 1.0)
        power = power * power
        lift = lift * jnp.where((seg_at // 2) % 2 == 1, power, 1.0)
        power = power * power
        lift = lift * jnp.where(seg_at // 4 == 1, power, 1.0)
        first = jnp.stack([jnp.broadcast_to(before[m : m + 1, g * LANES : (g + 1) * LANES], (8, LANES)) for m in range(MODES)])
        gain = skip[:, lanes]

        def step(i, state):
            p = prod[g, pl.ds(i, 8, stride=SEG), :]
            state = lam * state + p[None]
            conv[g, pl.ds(i, 8, stride=SEG), :] = jnp.sum(coef * state, axis=0) + gain * p
            return state

        lax.fori_loop(0, SEG, step, starts[:, :, lanes] + lift * first, unroll=4)
        rounded = conv[g].astype(BF16).astype(F32)
        gbuf[t, :, lanes] = (q[:, lanes].astype(F32) * rounded).astype(BF16)
        if g % 2 == 1:
            p = g // 2
            have_g.add((0, 0, p))
            ref = g_piece((0, 0, p))
            remote(ref, ref, s_g, r_g.at[p], at(dzl=1)).start()
            gated_out[0] += 1
            issue_g()
            absorb_until(4.0 + 0.3 * p)

    limits[2] = len(Z_SEND)
    issue()

    def multiply(dx, dz, first=False):
        b = chip_block(dx, dz)
        for n in range(0, CHAN, 256):
            cols = pl.ds(n, 256)
            w = wbuf[pl.ds(2 * b, 2), :, cols].reshape(2 * KROWS, 256)
            total = jnp.dot(gbuf[b], w, preferred_element_type=F32)
            acc[:, cols] = total if first else acc[:, cols] + total

    def multiply_rows(dx, dz, core, first, rows, last=False):
        b = chip_block(dx, dz)
        depth = pl.ds(pl.multiple_of(core * KROWS + first, 256), rows)
        for n in range(0, CHAN, 256):
            cols = pl.ds(n, 256)
            w = wbuf[2 * b + core, pl.ds(first, rows), cols]
            total = acc[:, cols] + jnp.dot(gbuf[b, :, depth], w, preferred_element_type=F32)
            if last:
                out_ref[:, cols] = total.astype(BF16)
            else:
                acc[:, cols] = total

    done = set()
    blocks = [(0, 0), (1, 0), (3, 0), (0, 1), (1, 1), (3, 1), (2, 0)]

    def work(most):
        for b in [b for b in blocks if b not in done and grains(*b, 0, KROWS) <= have][:most]:
            if b != (0, 0):
                from_sibling(*b)
            multiply(*b, first=not done)
            done.add(b)

    waits = [NY + 4]
    while events:
        _, i, r = events.pop(0)
        if i < 3:
            absorb(i, r)
        elif i == 3:
            absorb_g(r)
        else:
            absorb_zl(r)
        if i >= 3:
            waits[0] -= 1
            if not waits[0]:
                own_in.wait()
                remote(w_hbm, wbuf.at[s + 1 - 2 * c], s_e.at[1], r_e.at[1], at(dc=1)).wait_recv()
        if not waits[0] and len(events) > 2:
            work(1)
    work(8)
    assert len(done) == 7
    multiply_rows(2, 1, c, 0, KROWS)
    for part in range(2):
        from_sibling(2, 1, part)
        multiply_rows(2, 1, 1 - c, part * KROWS // 2, KROWS // 2, last=part == 1)

    for copy in sent:
        copy.wait_send()
    assert rows_out[0] % KROWS == 0 and gated_out[0] % 4 == 0
    ref = wbuf.at[pl.ds(0, rows_out[0] // KROWS)]
    remote(ref, ref, s_w, r_w.at[0], at(dc=1)).wait_send()
    ref = gbuf.at[pl.ds(0, gated_out[0] // 4)]
    remote(ref, ref, s_g, r_g.at[0], at(dc=1)).wait_send()
    for ok, copy in later:
        pl.when(ok)(copy.wait_send)


def body(query_stream, key_stream, value_stream, decay_rate, residue, skip_gain, out_weight):
    dma = pltpu.SemaphoreType.DMA
    vm = pltpu.VMEM
    return pl.pallas_call(
        kernel,
        out_shape=pltpu.VMEM((ROWS, CHAN), BF16),
        in_specs=[pl.BlockSpec(memory_space=pl.ANY)] * 7,
        out_specs=pl.BlockSpec(memory_space=pltpu.VMEM),
        scratch_shapes=[
            vm((ROWS, CHAN), BF16), vm((ROWS, CHAN), BF16), vm((ROWS, CHAN), BF16),
            vm((MODES, CHAN), F32), vm((MODES, CHAN), F32), vm((1, CHAN), F32),
            vm((16, KROWS, CHAN), BF16), vm((8, ROWS, CHAN), BF16), vm((ROWS, CHAN), F32),
            vm((GROUPS, ROWS, LANES), F32), vm((GROUPS, ROWS, LANES), F32),
            vm((MODES, 8, CHAN), F32), vm((MODES, 8, CHAN), F32), vm((MODES, 8, CHAN), F32),
            vm((MODES, CHAN), F32), vm((MODES, CHAN), F32), vm((8, CHAN), F32), vm((4, 8, CHAN), F32),
            vm((8, CHAN), F32), vm((8, CHAN), F32), vm((8, CHAN), F32),
            vm((MODES, CHAN), F32), vm((MODES, CHAN), F32),
            dma((6,)), dma, dma((len(X_RIGHT),)), dma((len(X_LEFT),)), dma((len(Z_SEND),)), dma, dma((10,)), dma((NY,)), dma((NY,)), dma, dma((4,)),
            dma((3,)), dma((3,)), dma((5,)), dma((5,)),
        ],
        compiler_params=pltpu.CompilerParams(
            collective_id=0, has_side_effects=True, vmem_limit_bytes=56 << 20
        ),
        cost_estimate=pl.CostEstimate(flops=2 * ROWS * 8192 * CHAN, bytes_accessed=4 << 20, transcendentals=0),
        name="hyena",
    )(query_stream, key_stream, value_stream, decay_rate.T, residue.T, skip_gain[None], out_weight)


def solution(mesh):
    placed = (
        P("seq", "tp"),
        P("seq", "tp"),
        P("seq", "tp"),
        P("tp", None),
        P("tp", None),
        P("tp"),
        P("seq", "tp"),
    )
    return jax.shard_map(
        body, mesh=mesh, in_specs=placed, out_specs=P("seq", "tp"), check_vma=False
    )
```
